256 devices in a mesh: inter: 8 (over x_hi, y), intra: 8 (over z), head: 4 (over x_lo, core).
Axes of the slice: x: 4 (x_hi: 2, x_lo: 2; x = x_hi * 2 + x_lo), y: 4, z: 8, core: 2. Of those that a mesh axis runs over, the one named last changes fastest.
Arguments:
- queries: bfloat16 [32, 8192, 128], P('head', ('inter', 'intra')), parts along dimension 0, may hold values from -6 to 6
- outputs: bfloat16 [32, 8192, 128], P('head', ('inter', 'intra')), parts along dimension 0, may hold values from -6 to 6
- out_grad: bfloat16 [32, 8192, 128], P('head', ('inter', 'intra')), parts along dimension 0, may hold values from -6 to 6
- log_norm: float32 [32, 8192], P('head', ('inter', 'intra')), parts along dimension 0, may hold values from 4 to 9
- key_values: bfloat16 [8192, 512], P(('inter', 'intra'), 'head'), parts along dimension 1, may hold values from -6 to 6
- key_exponent: int32 [1024], P(('head', 'inter', 'intra')), parts along dimension 0, may hold values from -1 to 0
- value_values: bfloat16 [8192, 512], P(('inter', 'intra'), 'head'), parts along dimension 1, may hold values from -6 to 6
- value_exponent: int32 [1024], P(('head', 'inter', 'intra')), parts along dimension 0, may hold values from -2 to 1
- span_order: int32 [512], P('head'), parts along dimension 0, may hold values from 0 to 127, each once
Outputs:
- query_grad: bfloat16 [32, 8192, 128], P('head', ('inter', 'intra')), parts along dimension 0
- key_grad: bfloat16 [8192, 512], P(('inter', 'intra'), 'head'), parts along dimension 1
- value_grad: bfloat16 [8192, 512], P(('inter', 'intra'), 'head'), parts along dimension 1
The draws below stay inside these ranges and needn't reach their ends.
There are 4 independent parts, one for each index of `head`. The reference program is written for one: setup_inputs(seed, part) draws one part's arguments, and reference() takes and returns one part's arrays. A program takes and returns all parts, laid end to end along the dimension named above; each array names one. Nothing has to cross between parts.
Inputs may be any that keep to these rules, and one draw needn't show every extreme that they name: `span_order`: a permutation of 0 to 127.
All inputs are finite; a program needn't handle non-finite values.
Results may differ from the reference program's by a relative error of at most 0.0049.
Values may be sent and summed in bfloat16 or wider, within the bound.
A program may use at most 64 MiB of HBM per device.

```python
import math
import jax
import jax.numpy as jnp
from jax import lax

H = 8
HD = 128
TOK_DEV = 128
BLK = 32
TOKENS = 8192
SPANS = 128


def place_ends(result, key, low, high):
    longest = result.shape.index(max(result.shape))
    spots = []
    for shift in (0, 1):
        where = [jax.random.randint(jax.random.fold_in(key, axis), (), 0, length) for axis, length in enumerate(result.shape)]
        where[longest] = (where[longest] + shift) % result.shape[longest]
        spots.append(tuple(where))
    return result.at[spots[0]].set(low).at[spots[1]].set(high)


def shard_levels(key, dims, split, smallest, top_value):
    def one(dim, shards_of):
        heights = jax.random.uniform(jax.random.fold_in(jax.random.fold_in(key, 6), dim), (shards_of,), jnp.float32, smallest / len(split), top_value / len(split))
        return jnp.repeat(jnp.exp(heights), dims[dim] // shards_of).reshape((-1,) + (1,) * (len(dims) - dim - 1))

    level = one(*split[0])
    for cut in split[1:]:
        level = level * one(*cut)
    return level


def normal_values(rng, dims, spread, most, cuts=(), held_as=jnp.bfloat16):
    result = jax.random.normal(rng, dims, jnp.float32) * spread
    if len(cuts) > 0:
        result = shard_levels(rng, dims, cuts, -0.22, 0.18) * result
    return jnp.clip(result, min=-most, max=most).astype(held_as)


def setup_inputs(seed: int = 0, part: int = 0) -> dict:
    key_of = jax.random.split(jax.random.key(seed), 10)
    own_keys = jax.random.split(jax.random.fold_in(key_of[9], part), 10)
    return {
        "queries": normal_values(own_keys[0], (H, TOKENS, HD), 1.0, 6.0, ((1, 64),)),
        "outputs": normal_values(own_keys[1], (H, TOKENS, HD), 1.0, 6.0, ((1, 64),)),
        "out_grad": normal_values(own_keys[2], (H, TOKENS, HD), 1.0, 6.0, ((1, 64),)),
        "log_norm": jnp.clip(4.0 + 5.0 * jax.random.uniform(own_keys[3], (H, TOKENS), jnp.float32) ** shard_levels(own_keys[3], (H, TOKENS), ((1, 64),), -0.2, 0.2), 4.0, 9.0),
        "key_values": normal_values(own_keys[4], (TOKENS, HD), 1.0, 6.0, ((0, 64),)),
        "key_exponent": place_ends(jax.random.randint(own_keys[5], (TOKENS // BLK,), -1, 1), jax.random.fold_in(own_keys[5], 1), -1, 0).astype(jnp.int32),
        "value_values": normal_values(own_keys[6], (TOKENS, HD), 1.0, 6.0, ((0, 64),)),
        "value_exponent": place_ends(jax.random.randint(own_keys[7], (TOKENS // BLK,), -2, 2), jax.random.fold_in(own_keys[7], 1), -2, 1).astype(jnp.int32),
        "span_order": jax.random.permutation(own_keys[8], SPANS).astype(jnp.int32),
    }


def dequantize(stored, exponent):
    factor = jnp.exp2(jnp.repeat(exponent, BLK).astype(jnp.float32))
    return (stored.astype(jnp.float32) * factor[:, None]).astype(jnp.bfloat16)


def reference(queries, outputs, out_grad, log_norm, key_values, key_exponent, value_values, value_exponent, span_order):
    half = TOK_DEV // 2
    scale = HD ** -0.5
    keys = dequantize(key_values, key_exponent)
    values = dequantize(value_values, value_exponent)
    ids = jnp.arange(TOKENS, dtype=jnp.int32)
    position = span_order[ids // half] * half + ids % half
    query32 = queries.astype(jnp.float32)
    grad32 = out_grad.astype(jnp.float32)
    delta = jnp.sum(grad32 * outputs.astype(jnp.float32), -1)
    step_rows = math.gcd(TOKENS, 512)

    def advance(index, carry):
        query_acc, key_acc, value_acc = carry
        start = (index * step_rows).astype(jnp.int32)
        kblock = lax.dynamic_slice_in_dim(keys, start, step_rows, 0).astype(jnp.float32)
        vblock = lax.dynamic_slice_in_dim(values, start, step_rows, 0).astype(jnp.float32)
        kpos = lax.dynamic_slice_in_dim(position, start, step_rows, 0)
        scores = jnp.einsum('htd,kd->htk', query32, kblock) * scale
        live = kpos[None, None, :] <= position[None, :, None]
        probs = jnp.where(live, jnp.exp(scores - log_norm[:, :, None]), 0.0)
        probs_low = lax.optimization_barrier(probs.astype(jnp.bfloat16)).astype(jnp.float32)
        value_block = jnp.einsum('htk,htd->kd', probs_low, grad32)
        dprob = jnp.einsum('htd,kd->htk', grad32, vblock)
        dscore = lax.optimization_barrier((probs * (dprob - delta[:, :, None])).astype(jnp.bfloat16)).astype(jnp.float32)
        query_acc = query_acc + jnp.einsum('htk,kd->htd', dscore, kblock)
        key_block = jnp.einsum('htk,htd->kd', dscore, query32) * scale
        key_acc = lax.dynamic_update_slice_in_dim(key_acc, key_block, start, 0)
        value_acc = lax.dynamic_update_slice_in_dim(value_acc, value_block, start, 0)
        return query_acc, key_acc, value_acc

    init = (jnp.zeros((H, TOKENS, HD), jnp.float32), jnp.zeros((TOKENS, HD), jnp.float32), jnp.zeros((TOKENS, HD), jnp.float32))
    query_acc, key_acc, value_acc = lax.fori_loop(0, TOKENS // step_rows, advance, init)
    return (query_acc * scale).astype(jnp.bfloat16), key_acc.astype(jnp.bfloat16), value_acc.astype(jnp.bfloat16)
```

```python
import math

import jax
import jax.numpy as jnp
from jax import lax
from jax.experimental import pallas as pl
from jax.experimental.pallas import tpu as pltpu
from jax.sharding import PartitionSpec as P

MESH = pl.DeviceIdType.MESH
F32, BF16 = jnp.float32, jnp.bfloat16
NT = (((1,), (1,)), ((), ()))
NN = (((1,), (0,)), ((), ()))
TN = (((0,), (0,)), ((), ()))
ROWS = 128
HALF = 64
WIDTH = 128
UNIT = 512
NX, NY, NZ = 2, 4, 8
MASKED = -(2.0**100)

ORDER = (
    (0, 0), (0, 1), (7, 0), (1, 0),
    (7, 1), (1, 1), (6, 0), (2, 0),
    (6, 1), (2, 1), (5, 0), (3, 0),
    (5, 1), (3, 1), (4, 0), (4, 1),
)
GROUP = 4
PAIRS = (0, 1, 1, 0, 1, 2, 0, 1, 2, 2, 3, 3, 2, 3, 3)
GROUPS = (1, 0, 1, 2, 2, 0, 3, 3, 3, 2, 3, 2, 1, 1, 0)


def slot(rel, column):
    return ORDER.index((rel % NZ, column))


def packed(digits):
    return sum(d * 4**n for n, d in enumerate(digits))


def dot(a, b, dims):
    return lax.dot_general(a, b, dims, preferred_element_type=F32)


def in_three(x):
    high = x.astype(BF16).astype(F32)
    rest = x - high
    mid = rest.astype(BF16).astype(F32)
    return high, mid, (rest - mid).astype(BF16).astype(F32)


def kernel(
    q_in,
    do_in,
    o_in,
    lse_in,
    k_in,
    v_in,
    kexp,
    vexp,
    spans,
    dq_out,
    dk_out,
    dv_out,
    qb,
    dob,
    ext,
    aux,
    kv,
    kext,
    vext,
    dq,
    dkv,
    kvs,
    kvr,
    last,
    xr,
    dqs,
    dqr,
    load_sem,
    kv_send,
    kv_recv,
    q_send,
    q_recv,
    aux_send,
    aux_recv,
    red_send,
    red_recv,
    last_recv,
    x_send,
    x_recv,
    dq_send,
    dq_recv,
):
    scale = WIDTH**-0.5
    root = WIDTH**0.5
    factor = scale * math.log2(math.e)
    inter, z, head = lax.axis_index("inter"), lax.axis_index("intra"), lax.axis_index("head")
    x, y = inter // NY, inter % NY

    def at(dx, dy, dz):
        return ((x + dx) % NX) * NY + (y + dy) % NY, (z + dz) % NZ

    def device(dx, dy, dz):
        return (*at(dx, dy, dz), head)

    UP, DOWN, ACROSS = device(0, 1, 0), device(0, -1, 0), device(0, 2, 0)
    RIGHT, LEFT, OTHER = device(0, 0, 1), device(0, 0, -1), device(1, 0, 0)

    def rows(index, size):
        return pl.ds(index * size, size)

    loads = []
    for u in range(2):
        for n, (src, dst) in enumerate(((q_in, qb), (do_in, dob))):
            loads.append(
                pltpu.make_async_copy(src.at[rows(u, UNIT)], dst.at[rows(u, UNIT)], load_sem.at[u, n])
            )
            loads[-1].start()

    barrier = pltpu.get_barrier_semaphore()
    for peer in (UP, DOWN, ACROSS, RIGHT, LEFT, OTHER):
        pl.semaphore_signal(barrier, inc=1, device_id=peer, device_id_type=MESH)

    def power(e):
        return jnp.where(e == -2, 0.25, jnp.where(e == -1, 0.5, jnp.where(e == 0, 1.0, 2.0)))

    block = ROWS // 4
    for b in range(4):
        r = rows(b, block)
        kv[r, :WIDTH] = (k_in[r, :].astype(F32) * power(kexp[b])).astype(BF16)
        kv[r, WIDTH:] = (v_in[r, :].astype(F32) * power(vexp[b])).astype(BF16)

    pl.semaphore_wait(barrier, 6)

    pending = []

    def send(src, dst, ssem, rsem, peer):
        def copy():
            return pltpu.make_async_remote_copy(
                src_ref=src(), dst_ref=dst(), send_sem=ssem(), recv_sem=rsem(), device_id=peer, device_id_type=MESH
            )

        copy().start()
        pending.append(copy)

    def arrived(dst, rsem):
        pltpu.make_async_remote_copy(
            src_ref=dst, dst_ref=dst, send_sem=rsem, recv_sem=rsem, device_id=UP, device_id_type=MESH
        ).wait_recv()

    def kv_go(way, src, dst):
        peer = (RIGHT, LEFT, OTHER)[way]
        send(
            lambda: kv.at[rows(src, ROWS)],
            lambda: kv.at[rows(dst, ROWS)],
            lambda: kv_send.at[way, src],
            lambda: kv_recv.at[dst],
            peer,
        )

    def kv_here(rel, column):
        s = slot(rel, column)
        arrived(kv.at[rows(s, ROWS)], kv_recv.at[s])

    def kv_pass(rel, column):
        kv_here(rel, column)
        s = slot(rel, column)
        if rel > 4:
            kv_go(0, s, slot(rel - 1, column))
        else:
            kv_go(1, s, slot(rel + 1, column))

    def q_go(src, dst, index, peer):
        for n, buf in enumerate((qb, dob)):
            send(
                lambda buf=buf: buf.at[rows(src, UNIT)],
                lambda buf=buf: buf.at[rows(dst, UNIT)],
                lambda n=n: q_send.at[index, n],
                lambda n=n: q_recv.at[dst, n],
                peer,
            )

    def q_here(u):
        for n, buf in enumerate((qb, dob)):
            arrived(buf.at[rows(u, UNIT)], q_recv.at[u, n])

    kv_go(2, 0, 1)
    kv_go(0, 0, slot(7, 0))
    kv_go(1, 0, slot(1, 0))
    for copy in loads:
        copy.wait()
    q_go(0, 2, 0, DOWN)
    q_go(1, 3, 1, UP)

    aux[0, 0] = lse_in[...] * root
    ones = jnp.ones((8, WIDTH), BF16)
    for u in range(2):
        r = rows(u, UNIT)
        prod = dob[r, :].astype(F32) * o_in[r, :].astype(F32)
        high = prod.astype(BF16)
        low = (prod - high.astype(F32)).astype(BF16)
        total = dot(ones, high, NT) + dot(ones, low, NT)
        for h in range(4):
            aux[0, 1, 4 * u + h : 4 * u + h + 1, :] = total[0:1, h * ROWS : (h + 1) * ROWS]
    for n, (dst, peer) in enumerate(((2, UP), (1, DOWN), (3, ACROSS))):
        send(
            lambda: aux.at[0],
            lambda dst=dst: aux.at[dst],
            lambda n=n: aux_send.at[n],
            lambda dst=dst: aux_recv.at[dst],
            peer,
        )

    q_go(1, 4, 2, DOWN)
    q_go(0, 5, 3, UP)

    def build_ext(u, b, first_head):
        row = lax.broadcasted_iota(jnp.int32, (16, ROWS), 0)
        lane = lax.broadcasted_iota(jnp.int32, (16, ROWS), 1)
        member = jnp.where(row == 6 + 2 * b + lane // HALF, 1.0, 0.0)
        for h in range(4):
            hh = first_head + h
            parts = in_three(aux[b, 0, hh : hh + 1, :]) + in_three(aux[b, 1, hh : hh + 1, :])
            m = member
            for n, part in enumerate(parts):
                m = jnp.where(row == n, part, m)
            m = jnp.concatenate([m, jnp.zeros((ROWS - 16, ROWS), F32)], 0)
            ext[pl.ds(u * UNIT + h * ROWS, ROWS), :] = m.T.astype(BF16)

    lanes = lax.broadcasted_iota(jnp.int32, (ROWS, WIDTH), 1)
    upper = lax.broadcasted_iota(jnp.int32, (ROWS, WIDTH), 0) >= HALF
    q_span = jnp.full((ROWS, WIDTH), 2**20, jnp.int32)
    for b, dy in enumerate((0, 1, -1, 2)):
        i, k = at(0, dy, 0)
        for n in range(2):
            q_span = jnp.where(lanes == 6 + 2 * b + n, spans[2 * (i * NZ + k) + n], q_span)
    base = jnp.where(lanes < 3, -1.0, 0.0)

    def build_kext(s):
        rel, column = ORDER[s]
        i, k = at(column, 0, rel)
        first = 2 * (i * NZ + k)
        k_span = jnp.where(upper, spans[first + 1], spans[first])
        kext[rows(s, ROWS), :] = jnp.where(k_span > q_span, MASKED, base).astype(BF16)

    def tile(units, s0, ns, diagonal=False):
        nk = ns * ROWS
        r = pl.ds(s0 * ROWS, nk)
        k = kv[r, :WIDTH]
        ka = jnp.concatenate([k, kext[r, :]], 1)
        va = jnp.concatenate([kv[r, WIDTH:], vext[:nk, :]], 1)
        ru = pl.ds(units * 2 * UNIT, 2 * UNIT)
        q, do, e = qb[ru, :], dob[ru, :], ext[ru, :]
        scores = dot(ka, jnp.concatenate([q, e], 1), NT)
        diff = dot(va, jnp.concatenate([do, e], 1), NT)
        probs = jnp.exp2(scores * factor)
        if diagonal:
            a = lax.broadcasted_iota(jnp.int32, (nk, 2 * UNIT), 0)
            t = lax.broadcasted_iota(jnp.int32, (nk, 2 * UNIT), 1) % ROWS
            probs = jnp.where((a // HALF != t // HALF) | (a <= t), probs, 0.0)
        low = probs.astype(BF16)
        ds = (probs * diff).astype(BF16)
        dkv[r, WIDTH:] += dot(low, do, NN)
        dkv[r, :WIDTH] += dot(ds, q, NN)
        dq[ru, :] += dot(ds, k, TN)

    def reduce_go(rel, column):
        s = slot(rel, column)
        r = rows(s, ROWS)
        total = dkv[r, :]
        if not (rel == 4 or (rel, column) in ((5, 1), (3, 0))):
            arrived(kvr.at[r], red_recv.at[s])
            total = total + kvr[r, :].astype(F32)
        left = rel > 4 or (rel == 4 and column == 0)
        peer = LEFT if left else RIGHT
        if rel in (1, 7):
            dkv[r, :] = total
            n = 2 * column + (rel == 1)
            send(
                lambda: dkv.at[rows(s, ROWS)],
                lambda: last.at[rows(n, ROWS)],
                lambda: red_send.at[s],
                lambda: last_recv.at[n],
                peer,
            )
        else:
            kvs[r, :] = total.astype(BF16)
            dst = slot(rel + 1 if left else rel - 1, column)
            send(
                lambda: kvs.at[rows(s, ROWS)],
                lambda: kvr.at[rows(dst, ROWS)],
                lambda: red_send.at[s],
                lambda: red_recv.at[dst],
                peer,
            )

    def dq_go(u, peer):
        r = rows(u - 2, UNIT)
        dqs[r, :] = dq[rows(u, UNIT), :].astype(BF16)
        send(
            lambda: dqs.at[rows(u - 2, UNIT)],
            lambda: dqr.at[rows(u - 2, UNIT)],
            lambda: dq_send.at[u - 2],
            lambda: dq_recv.at[u - 2],
            peer,
        )

    def own_total(column):
        total = dkv[rows(column, ROWS), :]
        for n in (2 * column, 2 * column + 1):
            arrived(last.at[rows(n, ROWS)], last_recv.at[n])
            total = total + last[rows(n, ROWS), :]
        return total

    kv_here(0, 1)
    kv_go(0, 1, slot(7, 1))
    kv_go(1, 1, slot(1, 1))
    kv_pass(7, 0)
    kv_pass(1, 0)
    for s in range(16):
        build_kext(s)
    build_ext(0, 0, 0)
    build_ext(1, 0, 4)
    wide = lax.broadcasted_iota(jnp.int32, vext.shape, 1)
    vext[...] = jnp.where((wide >= 3) & (wide < 6), -1.0, 0.0).astype(BF16)
    dq[...] = jnp.zeros_like(dq)
    dkv[...] = jnp.zeros_like(dkv)
    tile(0, 0, 1, diagonal=True)
    tile(0, 1, 3)

    def before_0():
        for rel, column in ORDER[4:8]:
            kv_pass(rel, column)

    def before_1():
        for n in (1, 2):
            arrived(aux.at[n], aux_recv.at[n])
        q_go(0, 6, 4, ACROSS)
        q_go(1, 7, 5, ACROSS)
        q_here(2)
        q_here(3)
        build_ext(2, 1, 0)
        build_ext(3, 2, 4)

    def before_2():
        kv_pass(6, 1)
        kv_pass(2, 1)
        kv_pass(5, 0)
        kv_here(3, 0)

    def before_4():
        kv_pass(3, 1)

    def before_5():
        q_here(4)
        q_here(5)
        build_ext(4, 1, 4)
        build_ext(5, 2, 0)

    def before_6():
        kv_here(5, 1)
        kv_here(4, 0)
        kv_here(4, 1)

    def before_8():
        dq_go(2, UP)
        dq_go(3, DOWN)

    def before_10():
        arrived(aux.at[3], aux_recv.at[3])
        q_here(6)
        q_here(7)
        build_ext(6, 3, 0)
        build_ext(7, 3, 4)

    def before_11():
        for rel, column in ((4, 0), (4, 1), (5, 1)):
            reduce_go(rel, column)

    def before_12():
        for rel, column in ((3, 1), (3, 0), (5, 0), (6, 1), (2, 1)):
            reduce_go(rel, column)

    def before_13():
        dq_go(4, UP)
        dq_go(5, DOWN)

    def before_14():
        for rel, column in ((7, 1), (1, 1), (6, 0), (2, 0)):
            reduce_go(rel, column)

    between = {
        0: before_0,
        1: before_1,
        2: before_2,
        4: before_4,
        5: before_5,
        6: before_6,
        8: before_8,
        10: before_10,
        11: before_11,
        12: before_12,
        13: before_13,
        14: before_14,
    }

    def step(i, codes):
        pair, group = codes
        for n, act in between.items():
            pl.when(i == n)(act)
        tile(pair % 4, (group % 4) * GROUP, GROUP)
        return pair // 4, group // 4

    lax.fori_loop(0, len(PAIRS), step, (jnp.int32(packed(PAIRS)), jnp.int32(packed(GROUPS))))

    dq_go(6, ACROSS)
    dq_go(7, ACROSS)
    reduce_go(7, 0)
    reduce_go(1, 0)
    r = rows(1, ROWS)
    dkv[r, :] = own_total(1)
    send(lambda: dkv.at[rows(1, ROWS)], lambda: xr, lambda: x_send, lambda: x_recv, OTHER)
    mine = own_total(0)
    arrived(xr, x_recv)
    mine = mine + xr[...]
    dk_out[...] = (mine[:, :WIDTH] * scale).astype(BF16)
    dv_out[...] = mine[:, WIDTH:].astype(BF16)
    for u, terms in ((0, (2, 5, 6)), (1, (3, 4, 7))):
        total = dq[rows(u, UNIT), :]
        for n in terms:
            r = rows(n - 2, UNIT)
            arrived(dqr.at[r], dq_recv.at[n - 2])
            total = total + dqr[r, :].astype(F32)
        dq_out[rows(u, UNIT), :] = (total * scale).astype(BF16)
    for copy in pending:
        copy().wait_send()


def body(
    queries,
    outputs,
    out_grad,
    log_norm,
    key_values,
    key_exponent,
    value_values,
    value_exponent,
    span_order,
):
    heads, tokens, width = queries.shape
    flat = (heads * tokens, width)
    vmem = pl.BlockSpec(memory_space=pltpu.VMEM)
    smem = pl.BlockSpec(memory_space=pltpu.SMEM)
    hbm = pl.BlockSpec(memory_space=pl.ANY)
    dma = pltpu.SemaphoreType.DMA
    units = 8 * UNIT
    keys = 16 * ROWS
    query_grad, key_grad, value_grad = pl.pallas_call(
        kernel,
        out_shape=(
            jax.ShapeDtypeStruct(flat, BF16),
            jax.ShapeDtypeStruct((tokens, width), BF16),
            jax.ShapeDtypeStruct((tokens, width), BF16),
        ),
        in_specs=[hbm, hbm, vmem, vmem, vmem, vmem, smem, smem, smem],
        out_specs=(vmem, vmem, vmem),
        scratch_shapes=[
            pltpu.VMEM((units, width), BF16),
            pltpu.VMEM((units, width), BF16),
            pltpu.VMEM((units, width), BF16),
            pltpu.VMEM((4, 2, heads, tokens), F32),
            pltpu.VMEM((keys, 2 * width), BF16),
            pltpu.VMEM((keys, width), BF16),
            pltpu.VMEM((GROUP * ROWS, width), BF16),
            pltpu.VMEM((units, width), F32),
            pltpu.VMEM((keys, 2 * width), F32),
            pltpu.VMEM((keys, 2 * width), BF16),
            pltpu.VMEM((keys, 2 * width), BF16),
            pltpu.VMEM((4 * ROWS, 2 * width), F32),
            pltpu.VMEM((ROWS, 2 * width), F32),
            pltpu.VMEM((6 * UNIT, width), BF16),
            pltpu.VMEM((6 * UNIT, width), BF16),
            dma((2, 2)),
            dma((3, 16)),
            dma((16,)),
            dma((6, 2)),
            dma((8, 2)),
            dma((3,)),
            dma((4,)),
            dma((16,)),
            dma((16,)),
            dma((4,)),
            dma,
            dma,
            dma((6,)),
            dma((6,)),
        ],
        compiler_params=pltpu.CompilerParams(
            collective_id=0, has_side_effects=True, vmem_limit_bytes=56 * 2**20
        ),
        cost_estimate=pl.CostEstimate(
            flops=10 * heads * tokens * 64 * tokens * width,
            bytes_accessed=8 * heads * tokens * width,
            transcendentals=heads * tokens * 64 * tokens,
        ),
        name="attention_backward",
    )(
        queries.reshape(flat),
        out_grad.reshape(flat),
        outputs.reshape(flat),
        log_norm,
        key_values,
        value_values,
        key_exponent,
        value_exponent,
        span_order,
    )
    return query_grad.reshape(heads, tokens, width), key_grad, value_grad


def solution(mesh):
    return jax.shard_map(
        body,
        mesh=mesh,
        in_specs=(
            P("head", ("inter", "intra"), None),
            P("head", ("inter", "intra"), None),
            P("head", ("inter", "intra"), None),
            P("head", ("inter", "intra")),
            P(("inter", "intra"), "head"),
            P(("head", "inter", "intra")),
            P(("inter", "intra"), "head"),
            P(("head", "inter", "intra")),
            P("head"),
        ),
        out_specs=(
            P("head", ("inter", "intra"), None),
            P(("inter", "intra"), "head"),
            P(("inter", "intra"), "head"),
        ),
        check_vma=False,
    )
```

```python
import math

import jax
import jax.numpy as jnp
from jax import lax
from jax.experimental import pallas as pl
from jax.experimental.pallas import tpu as pltpu
from jax.sharding import PartitionSpec as P

MESH = pl.DeviceIdType.MESH
F32, BF16 = jnp.float32, jnp.bfloat16
NT = (((1,), (1,)), ((), ()))
NN = (((1,), (0,)), ((), ()))
TN = (((0,), (0,)), ((), ()))
ROWS = 128
HALF = 64
WIDTH = 128
UNIT = 512
NX, NY, NZ = 2, 4, 8
MASKED = -(2.0**100)

ORDER = (
    (0, 0), (0, 1), (7, 0), (1, 0),
    (7, 1), (1, 1), (6, 0), (2, 0),
    (6, 1), (2, 1), (5, 0), (3, 0),
    (5, 1), (3, 1), (4, 0), (4, 1),
)
GROUP = 4
PAIRS = (0, 1, 1, 0, 1, 2, 2, 0, 1, 2, 3, 3, 2, 3, 3)
GROUPS = (1, 0, 1, 2, 2, 0, 2, 3, 3, 3, 3, 2, 1, 1, 0)


def slot(rel, column):
    return ORDER.index((rel % NZ, column))


def packed(digits):
    return sum(d * 4**n for n, d in enumerate(digits))


def dot(a, b, dims):
    return lax.dot_general(a, b, dims, preferred_element_type=F32)


def in_three(x):
    high = x.astype(BF16).astype(F32)
    rest = x - high
    mid = rest.astype(BF16).astype(F32)
    return high, mid, (rest - mid).astype(BF16).astype(F32)


def kernel(
    q_in,
    do_in,
    o_in,
    lse_in,
    k_in,
    v_in,
    kexp,
    vexp,
    spans,
    dq_out,
    dk_out,
    dv_out,
    qb,
    dob,
    ext,
    aux,
    kv,
    kext,
    vext,
    dq,
    dkv,
    kvs,
    kvr,
    last,
    xr,
    dqs,
    dqr,
    load_sem,
    kv_send,
    kv_recv,
    q_send,
    q_recv,
    aux_send,
    aux_recv,
    red_send,
    red_recv,
    last_recv,
    x_send,
    x_recv,
    dq_send,
    dq_recv,
):
    scale = WIDTH**-0.5
    root = WIDTH**0.5
    factor = scale * math.log2(math.e)
    inter, z, head = lax.axis_index("inter"), lax.axis_index("intra"), lax.axis_index("head")
    x, y = inter // NY, inter % NY

    def at(dx, dy, dz):
        return ((x + dx) % NX) * NY + (y + dy) % NY, (z + dz) % NZ

    def device(dx, dy, dz):
        return (*at(dx, dy, dz), head)

    UP, DOWN, ACROSS = device(0, 1, 0), device(0, -1, 0), device(0, 2, 0)
    RIGHT, LEFT, OTHER = device(0, 0, 1), device(0, 0, -1), device(1, 0, 0)
    RIGHT2, LEFT2 = device(0, 0, 2), device(0, 0, -2)

    def rows(index, size):
        return pl.ds(index * size, size)

    loads = []
    for u in range(2):
        for n, (src, dst) in enumerate(((q_in, qb), (do_in, dob))):
            loads.append(
                pltpu.make_async_copy(src.at[rows(u, UNIT)], dst.at[rows(u, UNIT)], load_sem.at[u, n])
            )
            loads[-1].start()

    barrier = pltpu.get_barrier_semaphore()
    for peer in (UP, DOWN, ACROSS, RIGHT, LEFT, RIGHT2, LEFT2, OTHER):
        pl.semaphore_signal(barrier, inc=1, device_id=peer, device_id_type=MESH)

    def power(e):
        return jnp.where(e == -2, 0.25, jnp.where(e == -1, 0.5, jnp.where(e == 0, 1.0, 2.0)))

    block = ROWS // 4
    for b in range(4):
        r = rows(b, block)
        kv[r, :WIDTH] = (k_in[r, :].astype(F32) * power(kexp[b])).astype(BF16)
        kv[r, WIDTH:] = (v_in[r, :].astype(F32) * power(vexp[b])).astype(BF16)

    pl.semaphore_wait(barrier, 8)

    pending = []

    def send(src, dst, ssem, rsem, peer):
        def copy():
            return pltpu.make_async_remote_copy(
                src_ref=src(), dst_ref=dst(), send_sem=ssem(), recv_sem=rsem(), device_id=peer, device_id_type=MESH
            )

        copy().start()
        pending.append(copy)

    def arrived(dst, rsem):
        pltpu.make_async_remote_copy(
            src_ref=dst, dst_ref=dst, send_sem=rsem, recv_sem=rsem, device_id=UP, device_id_type=MESH
        ).wait_recv()

    def kv_go(way, src, dst):
        peer = (RIGHT, LEFT, OTHER, RIGHT2, LEFT2)[way]
        send(
            lambda: kv.at[rows(src, ROWS)],
            lambda: kv.at[rows(dst, ROWS)],
            lambda: kv_send.at[way, src],
            lambda: kv_recv.at[dst],
            peer,
        )

    def kv_here(rel, column):
        s = slot(rel, column)
        arrived(kv.at[rows(s, ROWS)], kv_recv.at[s])

    def kv_near(column):
        s = slot(0, column)
        for way, rel in ((0, 7), (1, 1), (3, 6), (4, 2)):
            kv_go(way, s, slot(rel, column))

    def kv_far(rel, column):
        kv_here(rel, column)
        s = slot(rel, column)
        if rel == 6:
            kv_go(0, s, slot(5, column))
            if column == 0:
                kv_go(3, s, slot(4, column))
        else:
            kv_go(1, s, slot(3, column))
            if column == 1:
                kv_go(4, s, slot(4, column))

    def q_go(src, dst, index, peer):
        for n, buf in enumerate((qb, dob)):
            send(
                lambda buf=buf: buf.at[rows(src, UNIT)],
                lambda buf=buf: buf.at[rows(dst, UNIT)],
                lambda n=n: q_send.at[index, n],
                lambda n=n: q_recv.at[dst, n],
                peer,
            )

    def q_here(u):
        for n, buf in enumerate((qb, dob)):
            arrived(buf.at[rows(u, UNIT)], q_recv.at[u, n])

    kv_go(2, 0, 1)
    kv_near(0)
    for copy in loads:
        copy.wait()
    q_go(0, 2, 0, DOWN)
    q_go(1, 3, 1, UP)

    aux[0, 0] = lse_in[...] * root
    ones = jnp.ones((8, WIDTH), BF16)
    for u in range(2):
        r = rows(u, UNIT)
        prod = dob[r, :].astype(F32) * o_in[r, :].astype(F32)
        high = prod.astype(BF16)
        low = (prod - high.astype(F32)).astype(BF16)
        total = dot(ones, high, NT) + dot(ones, low, NT)
        for h in range(4):
            aux[0, 1, 4 * u + h : 4 * u + h + 1, :] = total[0:1, h * ROWS : (h + 1) * ROWS]
    for n, (dst, peer) in enumerate(((2, UP), (1, DOWN), (3, ACROSS))):
        send(
            lambda: aux.at[0],
            lambda dst=dst: aux.at[dst],
            lambda n=n: aux_send.at[n],
            lambda dst=dst: aux_recv.at[dst],
            peer,
        )

    def build_ext(u, b, first_head):
        row = lax.broadcasted_iota(jnp.int32, (16, ROWS), 0)
        lane = lax.broadcasted_iota(jnp.int32, (16, ROWS), 1)
        member = jnp.where(row == 6 + 2 * b + lane // HALF, 1.0, 0.0)
        for h in range(4):
            hh = first_head + h
            parts = in_three(aux[b, 0, hh : hh + 1, :]) + in_three(aux[b, 1, hh : hh + 1, :])
            m = member
            for n, part in enumerate(parts):
                m = jnp.where(row == n, part, m)
            m = jnp.concatenate([m, jnp.zeros((ROWS - 16, ROWS), F32)], 0)
            ext[pl.ds(u * UNIT + h * ROWS, ROWS), :] = m.T.astype(BF16)

    def tile(units, s0, ns, diagonal=False):
        nk = ns * ROWS
        r = pl.ds(s0 * ROWS, nk)
        k = kv[r, :WIDTH]
        ka = jnp.concatenate([k, kext[r, :]], 1)
        va = jnp.concatenate([kv[r, WIDTH:], vext[:nk, :]], 1)
        ru = pl.ds(units * 2 * UNIT, 2 * UNIT)
        q, do, e = qb[ru, :], dob[ru, :], ext[ru, :]
        scores = dot(ka, jnp.concatenate([q, e], 1), NT)
        diff = dot(va, jnp.concatenate([do, e], 1), NT)
        probs = jnp.exp2(scores * factor)
        if diagonal:
            a = lax.broadcasted_iota(jnp.int32, (nk, 2 * UNIT), 0)
            t = lax.broadcasted_iota(jnp.int32, (nk, 2 * UNIT), 1) % ROWS
            probs = jnp.where((a // HALF != t // HALF) | (a <= t), probs, 0.0)
        low = probs.astype(BF16)
        ds = (probs * diff).astype(BF16)
        dkv[r, WIDTH:] += dot(low, do, NN)
        dkv[r, :WIDTH] += dot(ds, q, NN)
        dq[ru, :] += dot(ds, k, TN)

    def reduce_go(rel, column):
        s = slot(rel, column)
        r = rows(s, ROWS)
        total = dkv[r, :]
        if not (rel == 4 or (rel, column) in ((5, 1), (3, 0))):
            arrived(kvr.at[r], red_recv.at[s])
            total = total + kvr[r, :].astype(F32)
        left = rel > 4 or (rel == 4 and column == 0)
        peer = LEFT if left else RIGHT
        if rel in (1, 7):
            dkv[r, :] = total
            n = 2 * column + (rel == 1)
            send(
                lambda: dkv.at[rows(s, ROWS)],
                lambda: last.at[rows(n, ROWS)],
                lambda: red_send.at[s],
                lambda: last_recv.at[n],
                peer,
            )
        else:
            kvs[r, :] = total.astype(BF16)
            dst = slot(rel + 1 if left else rel - 1, column)
            send(
                lambda: kvs.at[rows(s, ROWS)],
                lambda: kvr.at[rows(dst, ROWS)],
                lambda: red_send.at[s],
                lambda: red_recv.at[dst],
                peer,
            )

    def dq_go(u, peer):
        r = rows(u - 2, UNIT)
        dqs[r, :] = dq[rows(u, UNIT), :].astype(BF16)
        send(
            lambda: dqs.at[rows(u - 2, UNIT)],
            lambda: dqr.at[rows(u - 2, UNIT)],
            lambda: dq_send.at[u - 2],
            lambda: dq_recv.at[u - 2],
            peer,
        )

    def own_total(column):
        total = dkv[rows(column, ROWS), :]
        for n in (2 * column, 2 * column + 1):
            arrived(last.at[rows(n, ROWS)], last_recv.at[n])
            total = total + last[rows(n, ROWS), :]
        return total

    lanes = lax.broadcasted_iota(jnp.int32, (ROWS, WIDTH), 1)
    upper = lax.broadcasted_iota(jnp.int32, (ROWS, WIDTH), 0) >= HALF
    q_span = jnp.full((ROWS, WIDTH), 2**20, jnp.int32)
    for b, dy in enumerate((0, 1, -1, 2)):
        i, k = at(0, dy, 0)
        for n in range(2):
            q_span = jnp.where(lanes == 6 + 2 * b + n, spans[2 * (i * NZ + k) + n], q_span)
    base = jnp.where(lanes < 3, -1.0, 0.0)

    def build_kext(s):
        rel, column = ORDER[s]
        i, k = at(column, 0, rel)
        first = 2 * (i * NZ + k)
        k_span = jnp.where(upper, spans[first + 1], spans[first])
        kext[rows(s, ROWS), :] = jnp.where(k_span > q_span, MASKED, base).astype(BF16)

    for s in range(16):
        build_kext(s)
    wide = lax.broadcasted_iota(jnp.int32, vext.shape, 1)
    vext[...] = jnp.where((wide >= 3) & (wide < 6), -1.0, 0.0).astype(BF16)
    dq[...] = jnp.zeros_like(dq)
    dkv[...] = jnp.zeros_like(dkv)

    build_ext(0, 0, 0)
    build_ext(1, 0, 4)
    tile(0, 0, 1, diagonal=True)
    kv_here(0, 1)
    kv_near(1)
    q_go(1, 4, 2, DOWN)
    q_go(0, 5, 3, UP)
    kv_here(7, 0)
    kv_here(1, 0)
    tile(0, 1, 3)

    def before_0():
        kv_far(6, 0)
        kv_far(2, 0)
        kv_here(7, 1)
        kv_here(1, 1)

    def before_1():
        q_here(2)
        q_go(2, 6, 4, DOWN)
        q_here(3)
        q_go(3, 7, 5, UP)
        for n in (1, 2):
            arrived(aux.at[n], aux_recv.at[n])
        build_ext(2, 1, 0)
        build_ext(3, 2, 4)

    def before_2():
        kv_far(6, 1)
        kv_far(2, 1)

    def before_3():
        kv_here(5, 0)
        kv_here(3, 0)

    def before_5():
        q_here(4)
        q_here(5)
        build_ext(4, 1, 4)
        build_ext(5, 2, 0)

    def before_7():
        for rel, column in ORDER[12:]:
            kv_here(rel, column)

    def before_9():
        dq_go(2, UP)
        dq_go(3, DOWN)

    def before_10():
        arrived(aux.at[3], aux_recv.at[3])
        q_here(6)
        q_here(7)
        build_ext(6, 3, 0)
        build_ext(7, 3, 4)

    def before_11():
        for rel, column in ((4, 0), (4, 1), (5, 1)):
            reduce_go(rel, column)

    def before_12():
        for rel, column in ((3, 1), (3, 0), (5, 0), (6, 1), (2, 1)):
            reduce_go(rel, column)

    def before_13():
        dq_go(4, UP)
        dq_go(5, DOWN)

    def before_14():
        for rel, column in ((6, 0), (2, 0), (7, 1), (1, 1)):
            reduce_go(rel, column)

    between = {
        0: before_0,
        1: before_1,
        2: before_2,
        3: before_3,
        5: before_5,
        7: before_7,
        9: before_9,
        10: before_10,
        11: before_11,
        12: before_12,
        13: before_13,
        14: before_14,
    }

    def step(i, codes):
        pair, group = codes
        for n, act in between.items():
            pl.when(i == n)(act)
        tile(pair % 4, (group % 4) * GROUP, GROUP)
        return pair // 4, group // 4

    lax.fori_loop(0, len(PAIRS), step, (jnp.int32(packed(PAIRS)), jnp.int32(packed(GROUPS))))

    reduce_go(7, 0)
    reduce_go(1, 0)
    dq_go(6, ACROSS)
    dq_go(7, ACROSS)
    r = rows(1, ROWS)
    dkv[r, :] = own_total(1)
    send(lambda: dkv.at[rows(1, ROWS)], lambda: xr, lambda: x_send, lambda: x_recv, OTHER)
    mine = own_total(0)
    arrived(xr, x_recv)
    mine = mine + xr[...]
    dk_out[...] = (mine[:, :WIDTH] * scale).astype(BF16)
    dv_out[...] = mine[:, WIDTH:].astype(BF16)
    for u, terms in ((0, (2, 5, 6)), (1, (3, 4, 7))):
        total = dq[rows(u, UNIT), :]
        for n in terms:
            r = rows(n - 2, UNIT)
            arrived(dqr.at[r], dq_recv.at[n - 2])
            total = total + dqr[r, :].astype(F32)
        dq_out[rows(u, UNIT), :] = (total * scale).astype(BF16)
    for copy in pending:
        copy().wait_send()


def hand_over(dq_in, dk_in, dv_in, dq_out, dk_out, dv_out, sems):
    copies = [
        pltpu.make_async_copy(src, dst, sems.at[n])
        for n, (src, dst) in enumerate(((dq_in, dq_out), (dk_in, dk_out), (dv_in, dv_out)))
    ]
    for copy in copies:
        copy.start()
    for copy in copies:
        copy.wait()


def body(
    queries,
    outputs,
    out_grad,
    log_norm,
    key_values,
    key_exponent,
    value_values,
    value_exponent,
    span_order,
):
    heads, tokens, width = queries.shape
    flat = (heads * tokens, width)
    vmem = pl.BlockSpec(memory_space=pltpu.VMEM)
    smem = pl.BlockSpec(memory_space=pltpu.SMEM)
    hbm = pl.BlockSpec(memory_space=pl.ANY)
    dma = pltpu.SemaphoreType.DMA
    units = 8 * UNIT
    keys = 16 * ROWS
    grads = (
        jax.ShapeDtypeStruct(flat, BF16),
        jax.ShapeDtypeStruct((tokens, width), BF16),
        jax.ShapeDtypeStruct((tokens, width), BF16),
    )
    held = pl.pallas_call(
        kernel,
        out_shape=grads,
        in_specs=[hbm, hbm, vmem, vmem, vmem, vmem, smem, smem, smem],
        out_specs=(vmem, vmem, vmem),
        scratch_shapes=[
            pltpu.VMEM((units, width), BF16),
            pltpu.VMEM((units, width), BF16),
            pltpu.VMEM((units, width), BF16),
            pltpu.VMEM((4, 2, heads, tokens), F32),
            pltpu.VMEM((keys, 2 * width), BF16),
            pltpu.VMEM((keys, width), BF16),
            pltpu.VMEM((GROUP * ROWS, width), BF16),
            pltpu.VMEM((units, width), F32),
            pltpu.VMEM((keys, 2 * width), F32),
            pltpu.VMEM((keys, 2 * width), BF16),
            pltpu.VMEM((keys, 2 * width), BF16),
            pltpu.VMEM((4 * ROWS, 2 * width), F32),
            pltpu.VMEM((ROWS, 2 * width), F32),
            pltpu.VMEM((6 * UNIT, width), BF16),
            pltpu.VMEM((6 * UNIT, width), BF16),
            dma((2, 2)),
            dma((5, 16)),
            dma((16,)),
            dma((6, 2)),
            dma((8, 2)),
            dma((3,)),
            dma((4,)),
            dma((16,)),
            dma((16,)),
            dma((4,)),
            dma,
            dma,
            dma((6,)),
            dma((6,)),
        ],
        compiler_params=pltpu.CompilerParams(
            collective_id=0, has_side_effects=True, vmem_limit_bytes=56 * 2**20
        ),
        cost_estimate=pl.CostEstimate(
            flops=10 * heads * tokens * 64 * tokens * width,
            bytes_accessed=8 * heads * tokens * width,
            transcendentals=heads * tokens * 64 * tokens,
        ),
        name="attention_backward",
    )(
        queries.reshape(flat),
        out_grad.reshape(flat),
        outputs.reshape(flat),
        log_norm,
        key_values,
        value_values,
        key_exponent,
        value_exponent,
        span_order,
    )
    query_grad, key_grad, value_grad = pl.pallas_call(
        hand_over,
        out_shape=grads,
        in_specs=[hbm] * 3,
        out_specs=(vmem, vmem, vmem),
        scratch_shapes=[dma((3,))],
        name="hand_over",
    )(*held)
    return query_grad.reshape(heads, tokens, width), key_grad, value_grad


def solution(mesh):
    return jax.shard_map(
        body,
        mesh=mesh,
        in_specs=(
            P("head", ("inter", "intra"), None),
            P("head", ("inter", "intra"), None),
            P("head", ("inter", "intra"), None),
            P("head", ("inter", "intra")),
            P(("inter", "intra"), "head"),
            P(("head", "inter", "intra")),
            P(("inter", "intra"), "head"),
            P(("head", "inter", "intra")),
            P("head"),
        ),
        out_specs=(
            P("head", ("inter", "intra"), None),
            P(("inter", "intra"), "head"),
            P(("inter", "intra"), "head"),
        ),
        check_vma=False,
    )
```

```python
import math

import jax
import jax.numpy as jnp
from jax import lax
from jax.experimental import pallas as pl
from jax.experimental.pallas import tpu as pltpu
from jax.sharding import PartitionSpec as P

MESH = pl.DeviceIdType.MESH
F32, BF16 = jnp.float32, jnp.bfloat16
NT = (((1,), (1,)), ((), ()))
NN = (((1,), (0,)), ((), ()))
TN = (((0,), (0,)), ((), ()))
ROWS = 128
HALF = 64
WIDTH = 128
UNIT = 512
NX, NY, NZ = 2, 4, 8
MASKED = -(2.0**100)

ORDER = (
    (0, 0), (0, 1), (7, 0), (1, 0),
    (7, 1), (1, 1), (6, 0), (2, 0),
    (6, 1), (2, 1), (5, 0), (3, 0),
    (5, 1), (3, 1), (4, 0), (4, 1),
)
GROUP = 4
PAIRS = (0, 1, 1, 0, 1, 2, 2, 0, 1, 2, 3, 3, 2, 3, 3)
GROUPS = (1, 0, 1, 2, 2, 0, 2, 3, 3, 3, 3, 2, 1, 1, 0)


def slot(rel, column):
    return ORDER.index((rel % NZ, column))


def packed(digits):
    return sum(d * 4**n for n, d in enumerate(digits))


def dot(a, b, dims):
    return lax.dot_general(a, b, dims, preferred_element_type=F32)


def in_three(x):
    high = x.astype(BF16).astype(F32)
    rest = x - high
    mid = rest.astype(BF16).astype(F32)
    return high, mid, (rest - mid).astype(BF16).astype(F32)


def kernel(
    q_in,
    do_in,
    o_in,
    lse_in,
    k_in,
    v_in,
    kexp,
    vexp,
    spans,
    dq_out,
    dk_out,
    dv_out,
    qb,
    dob,
    ext,
    aux,
    kv,
    kext,
    vext,
    dq,
    dkv,
    kvs,
    kvr,
    last,
    xr,
    dqs,
    dqr,
    load_sem,
    kv_send,
    kv_recv,
    q_send,
    q_recv,
    aux_send,
    aux_recv,
    red_send,
    red_recv,
    last_recv,
    x_send,
    x_recv,
    dq_send,
    dq_recv,
):
    scale = WIDTH**-0.5
    root = WIDTH**0.5
    factor = scale * math.log2(math.e)
    inter, z, head = lax.axis_index("inter"), lax.axis_index("intra"), lax.axis_index("head")
    x, y = inter // NY, inter % NY

    def at(dx, dy, dz):
        return ((x + dx) % NX) * NY + (y + dy) % NY, (z + dz) % NZ

    def device(dx, dy, dz):
        return (*at(dx, dy, dz), head)

    UP, DOWN, ACROSS = device(0, 1, 0), device(0, -1, 0), device(0, 2, 0)
    RIGHT, LEFT, OTHER = device(0, 0, 1), device(0, 0, -1), device(1, 0, 0)
    RIGHT2, LEFT2 = device(0, 0, 2), device(0, 0, -2)

    def rows(index, size):
        return pl.ds(index * size, size)

    loads = []
    for u in range(2):
        for n, (src, dst) in enumerate(((q_in, qb), (do_in, dob))):
            loads.append(
                pltpu.make_async_copy(src.at[rows(u, UNIT)], dst.at[rows(u, UNIT)], load_sem.at[u, n])
            )
            loads[-1].start()

    barrier = pltpu.get_barrier_semaphore()
    for peer in (UP, DOWN, ACROSS, RIGHT, LEFT, RIGHT2, LEFT2, OTHER):
        pl.semaphore_signal(barrier, inc=1, device_id=peer, device_id_type=MESH)

    def power(e):
        return jnp.where(e == -2, 0.25, jnp.where(e == -1, 0.5, jnp.where(e == 0, 1.0, 2.0)))

    block = ROWS // 4
    for b in range(4):
        r = rows(b, block)
        kv[r, :WIDTH] = (k_in[r, :].astype(F32) * power(kexp[b])).astype(BF16)
        kv[r, WIDTH:] = (v_in[r, :].astype(F32) * power(vexp[b])).astype(BF16)

    pl.semaphore_wait(barrier, 8)

    pending = []

    def send(src, dst, ssem, rsem, peer):
        def copy():
            return pltpu.make_async_remote_copy(
                src_ref=src(), dst_ref=dst(), send_sem=ssem(), recv_sem=rsem(), device_id=peer, device_id_type=MESH
            )

        copy().start()
        pending.append(copy)

    def arrived(dst, rsem):
        pltpu.make_async_remote_copy(
            src_ref=dst, dst_ref=dst, send_sem=rsem, recv_sem=rsem, device_id=UP, device_id_type=MESH
        ).wait_recv()

    def kv_go(way, src, dst):
        peer = (RIGHT, LEFT, OTHER, RIGHT2, LEFT2)[way]
        send(
            lambda: kv.at[rows(src, ROWS)],
            lambda: kv.at[rows(dst, ROWS)],
            lambda: kv_send.at[way, src],
            lambda: kv_recv.at[dst],
            peer,
        )

    def kv_here(rel, column):
        s = slot(rel, column)
        arrived(kv.at[rows(s, ROWS)], kv_recv.at[s])

    def kv_near(column):
        s = slot(0, column)
        for way, rel in ((0, 7), (1, 1), (3, 6), (4, 2)):
            kv_go(way, s, slot(rel, column))

    def kv_far(rel, column):
        kv_here(rel, column)
        s = slot(rel, column)
        if rel == 6:
            kv_go(0, s, slot(5, column))
            if column == 0:
                kv_go(3, s, slot(4, column))
        else:
            kv_go(1, s, slot(3, column))
            if column == 1:
                kv_go(4, s, slot(4, column))

    def q_go(src, dst, index, peer):
        for n, buf in enumerate((qb, dob)):
            send(
                lambda buf=buf: buf.at[rows(src, UNIT)],
                lambda buf=buf: buf.at[rows(dst, UNIT)],
                lambda n=n: q_send.at[index, n],
                lambda n=n: q_recv.at[dst, n],
                peer,
            )

    def q_here(u):
        for n, buf in enumerate((qb, dob)):
            arrived(buf.at[rows(u, UNIT)], q_recv.at[u, n])

    kv_go(2, 0, 1)
    kv_near(0)
    for copy in loads:
        copy.wait()
    q_go(0, 2, 0, DOWN)
    q_go(1, 3, 1, UP)

    aux[0, 0] = lse_in[...] * root
    ones = jnp.ones((8, WIDTH), BF16)
    for u in range(2):
        r = rows(u, UNIT)
        prod = dob[r, :].astype(F32) * o_in[r, :].astype(F32)
        high = prod.astype(BF16)
        low = (prod - high.astype(F32)).astype(BF16)
        total = dot(ones, high, NT) + dot(ones, low, NT)
        for h in range(4):
            aux[0, 1, 4 * u + h : 4 * u + h + 1, :] = total[0:1, h * ROWS : (h + 1) * ROWS]
    for n, (dst, peer) in enumerate(((2, UP), (1, DOWN), (3, ACROSS))):
        send(
            lambda: aux.at[0],
            lambda dst=dst: aux.at[dst],
            lambda n=n: aux_send.at[n],
            lambda dst=dst: aux_recv.at[dst],
            peer,
        )

    def build_ext(u, b, first_head):
        row = lax.broadcasted_iota(jnp.int32, (16, ROWS), 0)
        lane = lax.broadcasted_iota(jnp.int32, (16, ROWS), 1)
        member = jnp.where(row == 6 + 2 * b + lane // HALF, 1.0, 0.0)
        for h in range(4):
            hh = first_head + h
            parts = in_three(aux[b, 0, hh : hh + 1, :]) + in_three(aux[b, 1, hh : hh + 1, :])
            m = member
            for n, part in enumerate(parts):
                m = jnp.where(row == n, part, m)
            m = jnp.concatenate([m, jnp.zeros((ROWS - 16, ROWS), F32)], 0)
            ext[pl.ds(u * UNIT + h * ROWS, ROWS), :] = m.T.astype(BF16)

    def tile(units, s0, ns, diagonal=False):
        nk = ns * ROWS
        r = pl.ds(s0 * ROWS, nk)
        k = kv[r, :WIDTH]
        ka = jnp.concatenate([k, kext[r, :]], 1)
        va = jnp.concatenate([kv[r, WIDTH:], vext[:nk, :]], 1)
        ru = pl.ds(units * 2 * UNIT, 2 * UNIT)
        q, do, e = qb[ru, :], dob[ru, :], ext[ru, :]
        scores = dot(ka, jnp.concatenate([q, e], 1), NT)
        diff = dot(va, jnp.concatenate([do, e], 1), NT)
        probs = jnp.exp2(scores * factor)
        if diagonal:
            a = lax.broadcasted_iota(jnp.int32, (nk, 2 * UNIT), 0)
            t = lax.broadcasted_iota(jnp.int32, (nk, 2 * UNIT), 1) % ROWS
            probs = jnp.where((a // HALF != t // HALF) | (a <= t), probs, 0.0)
        low = probs.astype(BF16)
        ds = (probs * diff).astype(BF16)
        dkv[r, WIDTH:] += dot(low, do, NN)
        dkv[r, :WIDTH] += dot(ds, q, NN)
        dq[ru, :] += dot(ds, k, TN)

    def reduce_go(rel, column):
        s = slot(rel, column)
        r = rows(s, ROWS)
        total = dkv[r, :]
        if not (rel == 4 or (rel, column) in ((5, 1), (3, 0))):
            arrived(kvr.at[r], red_recv.at[s])
            total = total + kvr[r, :].astype(F32)
        left = rel > 4 or (rel == 4 and column == 0)
        peer = LEFT if left else RIGHT
        if rel in (1, 7):
            dkv[r, :] = total
            n = 2 * column + (rel == 1)
            send(
                lambda: dkv.at[rows(s, ROWS)],
                lambda: last.at[rows(n, ROWS)],
                lambda: red_send.at[s],
                lambda: last_recv.at[n],
                peer,
            )
        else:
            kvs[r, :] = total.astype(BF16)
            dst = slot(rel + 1 if left else rel - 1, column)
            send(
                lambda: kvs.at[rows(s, ROWS)],
                lambda: kvr.at[rows(dst, ROWS)],
                lambda: red_send.at[s],
                lambda: red_recv.at[dst],
                peer,
            )

    def dq_go(u, peer):
        r = rows(u - 2, UNIT)
        dqs[r, :] = dq[rows(u, UNIT), :].astype(BF16)
        send(
            lambda: dqs.at[rows(u - 2, UNIT)],
            lambda: dqr.at[rows(u - 2, UNIT)],
            lambda: dq_send.at[u - 2],
            lambda: dq_recv.at[u - 2],
            peer,
        )

    def own_total(column):
        total = dkv[rows(column, ROWS), :]
        for n in (2 * column, 2 * column + 1):
            arrived(last.at[rows(n, ROWS)], last_recv.at[n])
            total = total + last[rows(n, ROWS), :]
        return total

    lanes = lax.broadcasted_iota(jnp.int32, (ROWS, WIDTH), 1)
    upper = lax.broadcasted_iota(jnp.int32, (ROWS, WIDTH), 0) >= HALF
    q_span = jnp.full((ROWS, WIDTH), 2**20, jnp.int32)
    for b, dy in enumerate((0, 1, -1, 2)):
        i, k = at(0, dy, 0)
        for n in range(2):
            q_span = jnp.where(lanes == 6 + 2 * b + n, spans[2 * (i * NZ + k) + n], q_span)
    base = jnp.where(lanes < 3, -1.0, 0.0)

    def build_kext(s):
        rel, column = ORDER[s]
        i, k = at(column, 0, rel)
        first = 2 * (i * NZ + k)
        k_span = jnp.where(upper, spans[first + 1], spans[first])
        kext[rows(s, ROWS), :] = jnp.where(k_span > q_span, MASKED, base).astype(BF16)

    for s in range(16):
        build_kext(s)
    wide = lax.broadcasted_iota(jnp.int32, vext.shape, 1)
    vext[...] = jnp.where((wide >= 3) & (wide < 6), -1.0, 0.0).astype(BF16)
    dq[...] = jnp.zeros_like(dq)
    dkv[...] = jnp.zeros_like(dkv)

    build_ext(0, 0, 0)
    build_ext(1, 0, 4)
    tile(0, 0, 1, diagonal=True)
    kv_here(0, 1)
    kv_near(1)
    q_go(1, 4, 2, DOWN)
    q_go(0, 5, 3, UP)
    kv_here(7, 0)
    kv_here(1, 0)
    tile(0, 1, 3)

    def before_0():
        kv_far(6, 0)
        kv_far(2, 0)
        kv_here(7, 1)
        kv_here(1, 1)

    def before_1():
        q_here(2)
        q_go(2, 6, 4, DOWN)
        q_here(3)
        q_go(3, 7, 5, UP)
        for n in (1, 2):
            arrived(aux.at[n], aux_recv.at[n])
        build_ext(2, 1, 0)
        build_ext(3, 2, 4)

    def before_2():
        kv_far(6, 1)
        kv_far(2, 1)

    def before_3():
        kv_here(5, 0)
        kv_here(3, 0)

    def before_5():
        q_here(4)
        q_here(5)
        build_ext(4, 1, 4)
        build_ext(5, 2, 0)

    def before_7():
        for rel, column in ORDER[12:]:
            kv_here(rel, column)

    def before_9():
        dq_go(2, UP)
        dq_go(3, DOWN)

    def before_10():
        arrived(aux.at[3], aux_recv.at[3])
        q_here(6)
        q_here(7)
        build_ext(6, 3, 0)
        build_ext(7, 3, 4)

    def before_11():
        for rel, column in ((4, 0), (4, 1), (5, 1)):
            reduce_go(rel, column)

    def before_12():
        for rel, column in ((3, 1), (3, 0), (5, 0), (6, 1), (2, 1)):
            reduce_go(rel, column)

    def before_13():
        dq_go(4, UP)
        dq_go(5, DOWN)

    def before_14():
        for rel, column in ((6, 0), (2, 0), (7, 1), (1, 1)):
            reduce_go(rel, column)

    between = {
        0: before_0,
        1: before_1,
        2: before_2,
        3: before_3,
        5: before_5,
        7: before_7,
        9: before_9,
        10: before_10,
        11: before_11,
        12: before_12,
        13: before_13,
        14: before_14,
    }

    def step(i, codes):
        pair, group = codes
        for n, act in between.items():
            pl.when(i == n)(act)
        tile(pair % 4, (group % 4) * GROUP, GROUP)
        return pair // 4, group // 4

    lax.fori_loop(0, len(PAIRS), step, (jnp.int32(packed(PAIRS)), jnp.int32(packed(GROUPS))))

    reduce_go(7, 0)
    reduce_go(1, 0)
    dq_go(6, ACROSS)
    dq_go(7, ACROSS)
    r = rows(1, ROWS)
    dkv[r, :] = own_total(1)
    send(lambda: dkv.at[rows(1, ROWS)], lambda: xr, lambda: x_send, lambda: x_recv, OTHER)
    mine = own_total(0)
    for u, terms in ((0, (2, 5, 6)), (1, (3, 4, 7))):
        total = dq[rows(u, UNIT), :]
        for n in terms:
            r = rows(n - 2, UNIT)
            arrived(dqr.at[r], dq_recv.at[n - 2])
            total = total + dqr[r, :].astype(F32)
        dq_out[rows(u, UNIT), :] = (total * scale).astype(BF16)
    arrived(xr, x_recv)
    mine = mine + xr[...]
    dk_out[...] = (mine[:, :WIDTH] * scale).astype(BF16)
    dv_out[...] = mine[:, WIDTH:].astype(BF16)
    for copy in pending:
        copy().wait_send()


def hand_over(dq_in, dk_in, dv_in, dq_out, dk_out, dv_out, sems):
    copies = [
        pltpu.make_async_copy(src, dst, sems.at[n])
        for n, (src, dst) in enumerate(((dq_in, dq_out), (dk_in, dk_out), (dv_in, dv_out)))
    ]
    for copy in copies:
        copy.start()
    for copy in copies:
        copy.wait()


def body(
    queries,
    outputs,
    out_grad,
    log_norm,
    key_values,
    key_exponent,
    value_values,
    value_exponent,
    span_order,
):
    heads, tokens, width = queries.shape
    flat = (heads * tokens, width)
    vmem = pl.BlockSpec(memory_space=pltpu.VMEM)
    smem = pl.BlockSpec(memory_space=pltpu.SMEM)
    hbm = pl.BlockSpec(memory_space=pl.ANY)
    dma = pltpu.SemaphoreType.DMA
    units = 8 * UNIT
    keys = 16 * ROWS
    grads = (
        jax.ShapeDtypeStruct(flat, BF16),
        jax.ShapeDtypeStruct((tokens, width), BF16),
        jax.ShapeDtypeStruct((tokens, width), BF16),
    )
    held = pl.pallas_call(
        kernel,
        out_shape=grads,
        in_specs=[hbm, hbm, vmem, vmem, vmem, vmem, smem, smem, smem],
        out_specs=(vmem, vmem, vmem),
        scratch_shapes=[
            pltpu.VMEM((units, width), BF16),
            pltpu.VMEM((units, width), BF16),
            pltpu.VMEM((units, width), BF16),
            pltpu.VMEM((4, 2, heads, tokens), F32),
            pltpu.VMEM((keys, 2 * width), BF16),
            pltpu.VMEM((keys, width), BF16),
            pltpu.VMEM((GROUP * ROWS, width), BF16),
            pltpu.VMEM((units, width), F32),
            pltpu.VMEM((keys, 2 * width), F32),
            pltpu.VMEM((keys, 2 * width), BF16),
            pltpu.VMEM((keys, 2 * width), BF16),
            pltpu.VMEM((4 * ROWS, 2 * width), F32),
            pltpu.VMEM((ROWS, 2 * width), F32),
            pltpu.VMEM((6 * UNIT, width), BF16),
            pltpu.VMEM((6 * UNIT, width), BF16),
            dma((2, 2)),
            dma((5, 16)),
            dma((16,)),
            dma((6, 2)),
            dma((8, 2)),
            dma((3,)),
            dma((4,)),
            dma((16,)),
            dma((16,)),
            dma((4,)),
            dma,
            dma,
            dma((6,)),
            dma((6,)),
        ],
        compiler_params=pltpu.CompilerParams(
            collective_id=0, has_side_effects=True, vmem_limit_bytes=56 * 2**20
        ),
        cost_estimate=pl.CostEstimate(
            flops=10 * heads * tokens * 64 * tokens * width,
            bytes_accessed=8 * heads * tokens * width,
            transcendentals=heads * tokens * 64 * tokens,
        ),
        name="attention_backward",
    )(
        queries.reshape(flat),
        out_grad.reshape(flat),
        outputs.reshape(flat),
        log_norm,
        key_values,
        value_values,
        key_exponent,
        value_exponent,
        span_order,
    )
    query_grad, key_grad, value_grad = pl.pallas_call(
        hand_over,
        out_shape=grads,
        in_specs=[hbm] * 3,
        out_specs=(vmem, vmem, vmem),
        scratch_shapes=[dma((3,))],
        name="hand_over",
    )(*held)
    return query_grad.reshape(heads, tokens, width), key_grad, value_grad


def solution(mesh):
    return jax.shard_map(
        body,
        mesh=mesh,
        in_specs=(
            P("head", ("inter", "intra"), None),
            P("head", ("inter", "intra"), None),
            P("head", ("inter", "intra"), None),
            P("head", ("inter", "intra")),
            P(("inter", "intra"), "head"),
            P(("head", "inter", "intra")),
            P(("inter", "intra"), "head"),
            P(("head", "inter", "intra")),
            P("head"),
        ),
        out_specs=(
            P("head", ("inter", "intra"), None),
            P(("inter", "intra"), "head"),
            P(("inter", "intra"), "head"),
        ),
        check_vma=False,
    )
```

```python
import math

import jax
import jax.numpy as jnp
from jax import lax
from jax.experimental import pallas as pl
from jax.experimental.pallas import tpu as pltpu
from jax.sharding import PartitionSpec as P

MESH = pl.DeviceIdType.MESH
F32, BF16 = jnp.float32, jnp.bfloat16
NT = (((1,), (1,)), ((), ()))
NN = (((1,), (0,)), ((), ()))
TN = (((0,), (0,)), ((), ()))
ROWS = 128
HALF = 64
WIDTH = 128
UNIT = 512
NX, NY, NZ = 2, 4, 8
MASKED = -(2.0**100)

ORDER = (
    (0, 0), (0, 1), (7, 0), (1, 0),
    (7, 1), (1, 1), (6, 0), (2, 0),
    (6, 1), (2, 1), (5, 0), (3, 0),
    (5, 1), (3, 1), (4, 0), (4, 1),
)
GROUP = 4
PAIRS = (0, 1, 1, 0, 1, 2, 2, 0, 1, 2, 3, 3, 2, 3, 3)
GROUPS = (1, 0, 1, 2, 2, 0, 2, 3, 3, 3, 3, 2, 1, 1, 0)


def slot(rel, column):
    return ORDER.index((rel % NZ, column))


def packed(digits):
    return sum(d * 4**n for n, d in enumerate(digits))


def dot(a, b, dims):
    return lax.dot_general(a, b, dims, preferred_element_type=F32)


def in_three(x):
    high = x.astype(BF16).astype(F32)
    rest = x - high
    mid = rest.astype(BF16).astype(F32)
    return high, mid, (rest - mid).astype(BF16).astype(F32)


def kernel(
    q_in,
    do_in,
    o_in,
    lse_in,
    k_in,
    v_in,
    kexp,
    vexp,
    spans,
    dq_out,
    dk_out,
    dv_out,
    qb,
    dob,
    ext,
    aux,
    kv,
    kext,
    vext,
    dq,
    dkv,
    kvs,
    kvr,
    last,
    xr,
    dqs,
    dqr,
    load_sem,
    kv_send,
    kv_recv,
    q_send,
    q_recv,
    aux_send,
    aux_recv,
    red_send,
    red_recv,
    last_recv,
    x_send,
    x_recv,
    dq_send,
    dq_recv,
):
    scale = WIDTH**-0.5
    root = WIDTH**0.5
    factor = scale * math.log2(math.e)
    inter, z, head = lax.axis_index("inter"), lax.axis_index("intra"), lax.axis_index("head")
    x, y = inter // NY, inter % NY

    def at(dx, dy, dz):
        return ((x + dx) % NX) * NY + (y + dy) % NY, (z + dz) % NZ

    def device(dx, dy, dz):
        return (*at(dx, dy, dz), head)

    UP, DOWN, ACROSS = device(0, 1, 0), device(0, -1, 0), device(0, 2, 0)
    RIGHT, LEFT, OTHER = device(0, 0, 1), device(0, 0, -1), device(1, 0, 0)
    RIGHT2, LEFT2 = device(0, 0, 2), device(0, 0, -2)
    OTHER_RIGHT, OTHER_LEFT = device(1, 0, 1), device(1, 0, -1)

    def rows(index, size):
        return pl.ds(index * size, size)

    loads = []
    for u in range(2):
        for n, (src, dst) in enumerate(((q_in, qb), (do_in, dob))):
            loads.append(
                pltpu.make_async_copy(src.at[rows(u, UNIT)], dst.at[rows(u, UNIT)], load_sem.at[u, n])
            )
            loads[-1].start()

    barrier = pltpu.get_barrier_semaphore()
    for peer in (UP, DOWN, ACROSS, RIGHT, LEFT, RIGHT2, LEFT2, OTHER, OTHER_RIGHT, OTHER_LEFT):
        pl.semaphore_signal(barrier, inc=1, device_id=peer, device_id_type=MESH)

    def power(e):
        return jnp.where(e == -2, 0.25, jnp.where(e == -1, 0.5, jnp.where(e == 0, 1.0, 2.0)))

    block = ROWS // 4
    for b in range(4):
        r = rows(b, block)
        kv[r, :WIDTH] = (k_in[r, :].astype(F32) * power(kexp[b])).astype(BF16)
        kv[r, WIDTH:] = (v_in[r, :].astype(F32) * power(vexp[b])).astype(BF16)

    pl.semaphore_wait(barrier, 10)

    pending = []

    def send(src, dst, ssem, rsem, peer):
        def copy():
            return pltpu.make_async_remote_copy(
                src_ref=src(), dst_ref=dst(), send_sem=ssem(), recv_sem=rsem(), device_id=peer, device_id_type=MESH
            )

        copy().start()
        pending.append(copy)

    def arrived(dst, rsem):
        pltpu.make_async_remote_copy(
            src_ref=dst, dst_ref=dst, send_sem=rsem, recv_sem=rsem, device_id=UP, device_id_type=MESH
        ).wait_recv()

    def kv_go(way, src, dst):
        peer = (RIGHT, LEFT, OTHER, RIGHT2, LEFT2, OTHER_RIGHT, OTHER_LEFT)[way]
        send(
            lambda: kv.at[rows(src, ROWS)],
            lambda: kv.at[rows(dst, ROWS)],
            lambda: kv_send.at[way, src],
            lambda: kv_recv.at[dst],
            peer,
        )

    def kv_here(rel, column):
        s = slot(rel, column)
        arrived(kv.at[rows(s, ROWS)], kv_recv.at[s])

    def kv_near(column):
        s = slot(0, column)
        if column == 0:
            kv_go(0, s, slot(7, 0))
            kv_go(1, s, slot(1, 0))
            kv_go(5, s, slot(7, 1))
            kv_go(6, s, slot(1, 1))
        kv_go(3, s, slot(6, column))
        kv_go(4, s, slot(2, column))

    def kv_far(rel, column):
        kv_here(rel, column)
        s = slot(rel, column)
        if rel == 6:
            kv_go(0, s, slot(5, column))
            if column == 0:
                kv_go(3, s, slot(4, column))
        else:
            kv_go(1, s, slot(3, column))
            if column == 1:
                kv_go(4, s, slot(4, column))

    def q_go(src, dst, index, peer):
        for n, buf in enumerate((qb, dob)):
            send(
                lambda buf=buf: buf.at[rows(src, UNIT)],
                lambda buf=buf: buf.at[rows(dst, UNIT)],
                lambda n=n: q_send.at[index, n],
                lambda n=n: q_recv.at[dst, n],
                peer,
            )

    def q_here(u):
        for n, buf in enumerate((qb, dob)):
            arrived(buf.at[rows(u, UNIT)], q_recv.at[u, n])

    kv_go(2, 0, 1)
    kv_near(0)
    for copy in loads:
        copy.wait()
    q_go(0, 2, 0, DOWN)
    q_go(1, 3, 1, UP)

    aux[0, 0] = lse_in[...] * root
    ones = jnp.ones((8, WIDTH), BF16)
    for u in range(2):
        r = rows(u, UNIT)
        prod = dob[r, :].astype(F32) * o_in[r, :].astype(F32)
        high = prod.astype(BF16)
        low = (prod - high.astype(F32)).astype(BF16)
        total = dot(ones, high, NT) + dot(ones, low, NT)
        for h in range(4):
            aux[0, 1, 4 * u + h : 4 * u + h + 1, :] = total[0:1, h * ROWS : (h + 1) * ROWS]
    for n, (dst, peer) in enumerate(((2, UP), (1, DOWN), (3, ACROSS))):
        send(
            lambda: aux.at[0],
            lambda dst=dst: aux.at[dst],
            lambda n=n: aux_send.at[n],
            lambda dst=dst: aux_recv.at[dst],
            peer,
        )

    def build_ext(u, b, first_head):
        row = lax.broadcasted_iota(jnp.int32, (16, ROWS), 0)
        lane = lax.broadcasted_iota(jnp.int32, (16, ROWS), 1)
        member = jnp.where(row == 6 + 2 * b + lane // HALF, 1.0, 0.0)
        for h in range(4):
            hh = first_head + h
            parts = in_three(aux[b, 0, hh : hh + 1, :]) + in_three(aux[b, 1, hh : hh + 1, :])
            m = member
            for n, part in enumerate(parts):
                m = jnp.where(row == n, part, m)
            m = jnp.concatenate([m, jnp.zeros((ROWS - 16, ROWS), F32)], 0)
            ext[pl.ds(u * UNIT + h * ROWS, ROWS), :] = m.T.astype(BF16)

    def tile(units, s0, ns, diagonal=False):
        nk = ns * ROWS
        r = pl.ds(s0 * ROWS, nk)
        k = kv[r, :WIDTH]
        ka = jnp.concatenate([k, kext[r, :]], 1)
        va = jnp.concatenate([kv[r, WIDTH:], vext[:nk, :]], 1)
        ru = pl.ds(units * 2 * UNIT, 2 * UNIT)
        q, do, e = qb[ru, :], dob[ru, :], ext[ru, :]
        scores = dot(ka, jnp.concatenate([q, e], 1), NT)
        diff = dot(va, jnp.concatenate([do, e], 1), NT)
        probs = jnp.exp2(scores * factor)
        if diagonal:
            a = lax.broadcasted_iota(jnp.int32, (nk, 2 * UNIT), 0)
            t = lax.broadcasted_iota(jnp.int32, (nk, 2 * UNIT), 1) % ROWS
            probs = jnp.where((a // HALF != t // HALF) | (a <= t), probs, 0.0)
        low = probs.astype(BF16)
        ds = (probs * diff).astype(BF16)
        dkv[r, WIDTH:] += dot(low, do, NN)
        dkv[r, :WIDTH] += dot(ds, q, NN)
        dq[ru, :] += dot(ds, k, TN)

    def reduce_go(rel, column):
        s = slot(rel, column)
        r = rows(s, ROWS)
        total = dkv[r, :]
        if not (rel == 4 or (rel, column) in ((5, 1), (3, 0))):
            arrived(kvr.at[r], red_recv.at[s])
            total = total + kvr[r, :].astype(F32)
        left = rel > 4 or (rel == 4 and column == 0)
        peer = LEFT if left else RIGHT
        if rel in (1, 7):
            dkv[r, :] = total
            n = 2 * column + (rel == 1)
            send(
                lambda: dkv.at[rows(s, ROWS)],
                lambda: last.at[rows(n, ROWS)],
                lambda: red_send.at[s],
                lambda: last_recv.at[n],
                peer,
            )
        else:
            kvs[r, :] = total.astype(BF16)
            dst = slot(rel + 1 if left else rel - 1, column)
            send(
                lambda: kvs.at[rows(s, ROWS)],
                lambda: kvr.at[rows(dst, ROWS)],
                lambda: red_send.at[s],
                lambda: red_recv.at[dst],
                peer,
            )

    def dq_go(u, peer):
        r = rows(u - 2, UNIT)
        dqs[r, :] = dq[rows(u, UNIT), :].astype(BF16)
        send(
            lambda: dqs.at[rows(u - 2, UNIT)],
            lambda: dqr.at[rows(u - 2, UNIT)],
            lambda: dq_send.at[u - 2],
            lambda: dq_recv.at[u - 2],
            peer,
        )

    def own_total(column):
        total = dkv[rows(column, ROWS), :]
        for n in (2 * column, 2 * column + 1):
            arrived(last.at[rows(n, ROWS)], last_recv.at[n])
            total = total + last[rows(n, ROWS), :]
        return total

    lanes = lax.broadcasted_iota(jnp.int32, (ROWS, WIDTH), 1)
    upper = lax.broadcasted_iota(jnp.int32, (ROWS, WIDTH), 0) >= HALF
    q_span = jnp.full((ROWS, WIDTH), 2**20, jnp.int32)
    for b, dy in enumerate((0, 1, -1, 2)):
        i, k = at(0, dy, 0)
        for n in range(2):
            q_span = jnp.where(lanes == 6 + 2 * b + n, spans[2 * (i * NZ + k) + n], q_span)
    base = jnp.where(lanes < 3, -1.0, 0.0)

    def build_kext(s):
        rel, column = ORDER[s]
        i, k = at(column, 0, rel)
        first = 2 * (i * NZ + k)
        k_span = jnp.where(upper, spans[first + 1], spans[first])
        kext[rows(s, ROWS), :] = jnp.where(k_span > q_span, MASKED, base).astype(BF16)

    for s in range(16):
        build_kext(s)
    wide = lax.broadcasted_iota(jnp.int32, vext.shape, 1)
    vext[...] = jnp.where((wide >= 3) & (wide < 6), -1.0, 0.0).astype(BF16)
    dq[...] = jnp.zeros_like(dq)
    dkv[...] = jnp.zeros_like(dkv)

    build_ext(0, 0, 0)
    build_ext(1, 0, 4)
    tile(0, 0, 1, diagonal=True)
    kv_here(0, 1)
    kv_near(1)
    q_go(1, 4, 2, DOWN)
    q_go(0, 5, 3, UP)
    kv_here(7, 0)
    kv_here(1, 0)
    tile(0, 1, 3)

    def before_0():
        kv_far(6, 0)
        kv_far(2, 0)
        kv_here(7, 1)
        kv_here(1, 1)

    def before_1():
        q_here(2)
        q_go(2, 6, 4, DOWN)
        q_here(3)
        q_go(3, 7, 5, UP)
        for n in (1, 2):
            arrived(aux.at[n], aux_recv.at[n])
        build_ext(2, 1, 0)
        build_ext(3, 2, 4)

    def before_2():
        kv_far(6, 1)
        kv_far(2, 1)

    def before_3():
        kv_here(5, 0)
        kv_here(3, 0)

    def before_5():
        q_here(4)
        q_here(5)
        build_ext(4, 1, 4)
        build_ext(5, 2, 0)

    def before_7():
        for rel, column in ORDER[12:]:
            kv_here(rel, column)

    def before_9():
        dq_go(2, UP)
        dq_go(3, DOWN)

    def before_10():
        arrived(aux.at[3], aux_recv.at[3])
        q_here(6)
        q_here(7)
        build_ext(6, 3, 0)
        build_ext(7, 3, 4)

    def before_11():
        for rel, column in ((4, 0), (4, 1), (5, 1)):
            reduce_go(rel, column)

    def before_12():
        for rel, column in ((3, 1), (3, 0), (5, 0), (6, 1), (2, 1)):
            reduce_go(rel, column)

    def before_13():
        dq_go(4, UP)
        dq_go(5, DOWN)

    def before_14():
        for rel, column in ((6, 0), (2, 0), (7, 1), (1, 1)):
            reduce_go(rel, column)

    between = {
        0: before_0,
        1: before_1,
        2: before_2,
        3: before_3,
        5: before_5,
        7: before_7,
        9: before_9,
        10: before_10,
        11: before_11,
        12: before_12,
        13: before_13,
        14: before_14,
    }

    def step(i, codes):
        pair, group = codes
        for n, act in between.items():
            pl.when(i == n)(act)
        tile(pair % 4, (group % 4) * GROUP, GROUP)
        return pair // 4, group // 4

    lax.fori_loop(0, len(PAIRS), step, (jnp.int32(packed(PAIRS)), jnp.int32(packed(GROUPS))))

    reduce_go(7, 0)
    reduce_go(1, 0)
    dq_go(6, ACROSS)
    dq_go(7, ACROSS)
    r = rows(1, ROWS)
    dkv[r, :] = own_total(1)
    send(lambda: dkv.at[rows(1, ROWS)], lambda: xr, lambda: x_send, lambda: x_recv, OTHER)
    mine = own_total(0)
    for u, terms in ((0, (2, 5, 6)), (1, (3, 4, 7))):
        total = dq[rows(u, UNIT), :]
        for n in terms:
            r = rows(n - 2, UNIT)
            arrived(dqr.at[r], dq_recv.at[n - 2])
            total = total + dqr[r, :].astype(F32)
        dq_out[rows(u, UNIT), :] = (total * scale).astype(BF16)
    arrived(xr, x_recv)
    mine = mine + xr[...]
    dk_out[...] = (mine[:, :WIDTH] * scale).astype(BF16)
    dv_out[...] = mine[:, WIDTH:].astype(BF16)
    for copy in pending:
        copy().wait_send()


def hand_over(dq_in, dk_in, dv_in, dq_out, dk_out, dv_out, sems):
    copies = [
        pltpu.make_async_copy(src, dst, sems.at[n])
        for n, (src, dst) in enumerate(((dq_in, dq_out), (dk_in, dk_out), (dv_in, dv_out)))
    ]
    for copy in copies:
        copy.start()
    for copy in copies:
        copy.wait()


def body(
    queries,
    outputs,
    out_grad,
    log_norm,
    key_values,
    key_exponent,
    value_values,
    value_exponent,
    span_order,
):
    heads, tokens, width = queries.shape
    flat = (heads * tokens, width)
    vmem = pl.BlockSpec(memory_space=pltpu.VMEM)
    smem = pl.BlockSpec(memory_space=pltpu.SMEM)
    hbm = pl.BlockSpec(memory_space=pl.ANY)
    dma = pltpu.SemaphoreType.DMA
    units = 8 * UNIT
    keys = 16 * ROWS
    grads = (
        jax.ShapeDtypeStruct(flat, BF16),
        jax.ShapeDtypeStruct((tokens, width), BF16),
        jax.ShapeDtypeStruct((tokens, width), BF16),
    )
    held = pl.pallas_call(
        kernel,
        out_shape=grads,
        in_specs=[hbm, hbm, vmem, vmem, vmem, vmem, smem, smem, smem],
        out_specs=(vmem, vmem, vmem),
        scratch_shapes=[
            pltpu.VMEM((units, width), BF16),
            pltpu.VMEM((units, width), BF16),
            pltpu.VMEM((units, width), BF16),
            pltpu.VMEM((4, 2, heads, tokens), F32),
            pltpu.VMEM((keys, 2 * width), BF16),
            pltpu.VMEM((keys, width), BF16),
            pltpu.VMEM((GROUP * ROWS, width), BF16),
            pltpu.VMEM((units, width), F32),
            pltpu.VMEM((keys, 2 * width), F32),
            pltpu.VMEM((keys, 2 * width), BF16),
            pltpu.VMEM((keys, 2 * width), BF16),
            pltpu.VMEM((4 * ROWS, 2 * width), F32),
            pltpu.VMEM((ROWS, 2 * width), F32),
            pltpu.VMEM((6 * UNIT, width), BF16),
            pltpu.VMEM((6 * UNIT, width), BF16),
            dma((2, 2)),
            dma((7, 16)),
            dma((16,)),
            dma((6, 2)),
            dma((8, 2)),
            dma((3,)),
            dma((4,)),
            dma((16,)),
            dma((16,)),
            dma((4,)),
            dma,
            dma,
            dma((6,)),
            dma((6,)),
        ],
        compiler_params=pltpu.CompilerParams(
            collective_id=0, has_side_effects=True, vmem_limit_bytes=56 * 2**20
        ),
        cost_estimate=pl.CostEstimate(
            flops=10 * heads * tokens * 64 * tokens * width,
            bytes_accessed=8 * heads * tokens * width,
            transcendentals=heads * tokens * 64 * tokens,
        ),
        name="attention_backward",
    )(
        queries.reshape(flat),
        out_grad.reshape(flat),
        outputs.reshape(flat),
        log_norm,
        key_values,
        value_values,
        key_exponent,
        value_exponent,
        span_order,
    )
    query_grad, key_grad, value_grad = pl.pallas_call(
        hand_over,
        out_shape=grads,
        in_specs=[hbm] * 3,
        out_specs=(vmem, vmem, vmem),
        scratch_shapes=[dma((3,))],
        name="hand_over",
    )(*held)
    return query_grad.reshape(heads, tokens, width), key_grad, value_grad


def solution(mesh):
    return jax.shard_map(
        body,
        mesh=mesh,
        in_specs=(
            P("head", ("inter", "intra"), None),
            P("head", ("inter", "intra"), None),
            P("head", ("inter", "intra"), None),
            P("head", ("inter", "intra")),
            P(("inter", "intra"), "head"),
            P(("head", "inter", "intra")),
            P(("inter", "intra"), "head"),
            P(("head", "inter", "intra")),
            P("head"),
        ),
        out_specs=(
            P("head", ("inter", "intra"), None),
            P(("inter", "intra"), "head"),
            P(("inter", "intra"), "head"),
        ),
        check_vma=False,
    )
```
